128 devices in a mesh: dp: 64 (over y, x, z_hi, core), tensor: 2 (over z_lo).
Axes of the slice: x: 4, y: 4, z: 4 (z_hi: 2, z_lo: 2; z = z_hi * 2 + z_lo), core: 2. Of those that a mesh axis runs over, the one named last changes fastest.
Arguments:
- tokens: bfloat16 [16384, 2048], P(('dp', 'tensor')), may hold values from -24 to 24
- seq_lengths: int32 [64, 3], P('dp'), may hold values from 1 to 170, 256 in all within a row
- attn_gain: float32 [2048], replicated, may hold values from 0.1 to 1.9
- wq: bfloat16 [2048, 2048], P('dp', 'tensor'), may hold values from -0.125 to 0.125
- wk: bfloat16 [2048, 512], P('dp', 'tensor'), may hold values from -0.125 to 0.125
- wv: bfloat16 [2048, 512], P('dp', 'tensor'), may hold values from -0.125 to 0.125
- wo: bfloat16 [2048, 2048], P('tensor', 'dp'), may hold values from -0.5 to 0.5
- mlp_gain: float32 [2048], replicated, may hold values from 0.1 to 1.9
- w_gate: bfloat16 [2048, 8192], P('dp', 'tensor'), may hold values from -0.125 to 0.125
- w_up: bfloat16 [2048, 8192], P('dp', 'tensor'), may hold values from -0.125 to 0.125
- w_down: bfloat16 [8192, 2048], P('tensor', 'dp'), may hold values from -0.09375 to 0.09375
- cotangent: bfloat16 [16384, 2048], P(('dp', 'tensor')), may hold values from -24 to 24
Outputs:
- layer_out: bfloat16 [16384, 2048], P(('dp', 'tensor'))
- tokens_grad: bfloat16 [16384, 2048], P(('dp', 'tensor'))
- attn_gain_grad: float32 [2048], P('dp')
- wq_grad: float32 [2048, 2048], P('dp', 'tensor')
- wk_grad: float32 [2048, 512], P('dp', 'tensor')
- wv_grad: float32 [2048, 512], P('dp', 'tensor')
- wo_grad: float32 [2048, 2048], P('tensor', 'dp')
- mlp_gain_grad: float32 [2048], P('dp')
- gate_grad: float32 [2048, 8192], P('dp', 'tensor')
- up_grad: float32 [2048, 8192], P('dp', 'tensor')
- down_grad: float32 [8192, 2048], P('tensor', 'dp')
The draws below stay inside these ranges and needn't reach their ends.
Inputs may be any that keep to these rules, and one draw needn't show every extreme that they name: `seq_lengths`: in each group the 3 lengths sum to 256, and one of them is exactly 170.
All inputs are finite; a program needn't handle non-finite values.
Results may differ from the reference program's by a relative error of at most 0.019.
Values may be sent and summed in bfloat16 or wider, within the bound.
No kernel may reach another device: no remote copies, remote signals or barrier semaphores. Data moves between devices by JAX's collectives and lax.ppermute only.
A program may use at most 256 MiB of HBM per device.

```python
import math
import jax
import jax.numpy as jnp
import numpy as np
from jax import lax

MODEL_WIDTH = 2048
QUERY_COUNT = 32
VALUE_HEADS = 8
HEAD_WIDTH = 64
FF = 8192
SEQS = 3
GROUP_TOK = 256
LONGEST = 170
TOKENS = 16384
N_DP = 64


def strengthened(values, key, source, target, shards_of, factor):
    owner, partner = [(jnp.arange(values.shape[axis_at]) // (values.shape[axis_at] // shards_of)).reshape([-1 if axis == axis_at else 1 for axis in range(values.ndim)]) for axis_at in (source, target)]
    chosen = jax.random.permutation(key, shards_of)[partner]
    strong = (owner == chosen) | (owner == (partner + shards_of // 2) % shards_of)
    return jnp.where(strong, factor * values, values)


def block_scale(stream_key, shape, cuts, low, high):
    factor_of, own = 1.0, jax.random.fold_in(stream_key, 6)
    for dim, shards_of in cuts:
        draws = jnp.exp(jax.random.uniform(jax.random.fold_in(own, dim), (shards_of,), jnp.float32, low / len(cuts), high / len(cuts)))
        factor_of = factor_of * jnp.repeat(draws, shape[dim] // shards_of).reshape([-1 if axis == dim else 1 for axis in range(len(shape))])
    return factor_of


def length_profile(number_of, total, most, slope):
    weights = [(1 << 20) // math.isqrt(rank ** slope) + 1 for rank in range(2, number_of + 1)]
    surplus, given = total - most - (number_of - 1), [1] * (number_of - 1)
    while surplus > 0:
        free = [i for i in range(number_of - 1) if given[i] < most]
        mass, remaining = sum([weights[i] for i in free]), surplus
        for i in free:
            addition = min(most - given[i], max(1, remaining * weights[i] // mass), surplus)
            given[i] = given[i] + addition
            surplus = surplus - addition
    return np.array([most] + given)


def ragged_sizes(own_key, count, total, most, slope):
    if count == 2:
        one = jax.random.randint(own_key, (), max(1, total - most), min(most, total - 1) + 1)
        return jnp.stack([one, total - one])
    sizes = jnp.asarray(length_profile(count, total, most, slope), jnp.int32)
    pairs = (count - 1) // 2
    source_of, taker = sizes[1:1 + 2 * pairs:2], sizes[2:2 + 2 * pairs:2]
    room = jnp.minimum(source_of - 1, most - taker)
    moved = jax.random.randint(jax.random.fold_in(own_key, 1), (pairs,), 0, 1 << 20) % (room + 1)
    sizes = sizes.at[1:1 + 2 * pairs:2].set(source_of - moved).at[2:2 + 2 * pairs:2].set(taker + moved)
    return sizes[jax.random.permutation(jax.random.fold_in(own_key, 2), count)]


def bell_draw(key, shape, spread, limit, pieces=(), kind=jnp.bfloat16):
    array = jax.random.normal(key, shape, jnp.float32) * spread
    if len(pieces) > 0:
        array = block_scale(key, shape, pieces, -0.22, 0.18) * array
    return jnp.clip(array, min=-limit, max=limit).astype(kind)


def bell_draw_with(key, shape, spread, bound, shards, heavy, kind=jnp.bfloat16):
    drawn = spread * jax.random.normal(key, shape, jnp.float32)
    if shards:
        drawn = drawn * block_scale(key, shape, shards, -0.22, 0.18)
    return jnp.clip(strengthened(drawn, jax.random.fold_in(key, 3), *heavy), -bound, bound).astype(kind)


def setup_inputs(seed: int = 0) -> dict:
    splits = jax.random.split(jax.random.key(seed), 13)
    tokens = bell_draw_with(splits[0], (TOKENS, MODEL_WIDTH), 1.0, 24.0, ((0, 128),), (0, 1, 128, 5.5))
    seq_lengths = jax.vmap(lambda own: ragged_sizes(own, SEQS, GROUP_TOK, LONGEST, 2))(jax.random.split(splits[1], N_DP)).reshape((N_DP, SEQS)).astype(jnp.int32)
    attn_gain = jnp.clip(1.0 + 0.18 * jax.random.normal(splits[2], (MODEL_WIDTH,), jnp.float32), 0.1, 1.9)
    wq = bell_draw(splits[3], (MODEL_WIDTH, QUERY_COUNT * HEAD_WIDTH), MODEL_WIDTH ** -0.5, 0.125, ((0, 64), (1, 2)))
    wk = bell_draw(splits[4], (MODEL_WIDTH, VALUE_HEADS * HEAD_WIDTH), MODEL_WIDTH ** -0.5, 0.125, ((0, 64), (1, 2)))
    wv = bell_draw(splits[5], (MODEL_WIDTH, VALUE_HEADS * HEAD_WIDTH), MODEL_WIDTH ** -0.5, 0.125, ((0, 64), (1, 2)))
    wo = bell_draw(splits[6], (QUERY_COUNT * HEAD_WIDTH, MODEL_WIDTH), (QUERY_COUNT * HEAD_WIDTH // 16) ** -0.5, 0.5, ((0, 2), (1, 64)))
    mlp_gain = jnp.clip(1.0 + 0.18 * jax.random.normal(splits[7], (MODEL_WIDTH,), jnp.float32), 0.1, 1.9)
    w_gate = bell_draw(splits[8], (MODEL_WIDTH, FF), MODEL_WIDTH ** -0.5, 0.125, ((0, 64), (1, 2)))
    w_up = bell_draw(splits[9], (MODEL_WIDTH, FF), MODEL_WIDTH ** -0.5, 0.125, ((0, 64), (1, 2)))
    w_down = bell_draw(splits[10], (FF, MODEL_WIDTH), (FF // 2) ** -0.5, 0.09375, ((0, 2), (1, 64)))
    cotangent = bell_draw_with(splits[11], (TOKENS, MODEL_WIDTH), 1.0, 24.0, ((0, 128),), (0, 1, 128, 5.5))
    return {"tokens": tokens, "seq_lengths": seq_lengths, "attn_gain": attn_gain, "wq": wq, "wk": wk, "wv": wv, "wo": wo, "mlp_gain": mlp_gain, "w_gate": w_gate, "w_up": w_up, "w_down": w_down, "cotangent": cotangent}


EPS = 1e-05
HIGH_PRECISION = lax.Precision.HIGHEST
NEG = -1e+30

@jax.custom_vjp
def low_precision(v):
    return lax.optimization_barrier(v.astype(jnp.bfloat16)).astype(jnp.float32)

@jax.custom_vjp
def lowered_backward(v):
    return v

def low_keep(v):
    return (low_precision(v), None)

def low_pass(kept, grad):
    return (grad,)

def back_keep(v):
    return (v, None)

def back_low(kept, grad):
    return (low_precision(grad),)
low_precision.defvjp(low_keep, low_pass)
lowered_backward.defvjp(back_keep, back_low)

def rotary_tables(positions, head_size):
    freq_index = jnp.arange(head_size // 2, dtype=jnp.float32)
    inverse = 1.0 / 500000.0 ** (2.0 * freq_index / head_size)
    wavelen = 2.0 * math.pi / inverse
    smooth = (8192.0 / wavelen - 1.0) / 3.0
    blended = (1.0 - smooth) * inverse / 32.0 + smooth * inverse
    scaled = jnp.where(wavelen > 8192.0, inverse / 32.0, jnp.where(wavelen < 2048.0, inverse, blended))
    angles = positions.astype(jnp.float32)[:, None] * scaled[None, :]
    cosine = jnp.cos(angles)
    sine_part = jnp.sin(angles)
    return (jnp.concatenate([cosine, cosine], -1), jnp.concatenate([sine_part, sine_part], -1))

def rotate_half(values):
    front_part = values[..., :values.shape[-1] // 2]
    back_part = values[..., values.shape[-1] // 2:]
    return jnp.concatenate([-back_part, front_part], -1)

def rope_apply(values, cosine, sine_part):
    return values * cosine[:, None, :] + rotate_half(values) * sine_part[:, None, :]

def segment_layout(lengths, row_number):
    seq_ends = jnp.cumsum(lengths).astype(jnp.int32)
    seq_starts = (seq_ends - lengths).astype(jnp.int32)
    row_index = jnp.arange(row_number, dtype=jnp.int32)
    segment_labels = lax.optimization_barrier(jnp.sum((row_index[:, None] >= seq_ends[None, :]).astype(jnp.int32), axis=1)).astype(jnp.int32)
    slot_index = jnp.arange(lengths.shape[0], dtype=jnp.int32)
    start_here = lax.optimization_barrier(jnp.sum(jnp.where(segment_labels[:, None] == slot_index[None, :], seq_starts[None, :], 0), axis=1))
    return (segment_labels, (row_index - start_here).astype(jnp.int32))

def rms_norm(values, gain_vector):
    return values * lax.rsqrt(lax.optimization_barrier(jnp.mean(values * values, axis=-1, keepdims=True)) + EPS) * gain_vector

def grouped_attention(queries, keys, values, segment_labels):
    row_number = queries.shape[0]
    group_size = queries.shape[1] // keys.shape[1]
    grouped = queries.reshape(row_number, keys.shape[1], group_size, HEAD_WIDTH)
    scores = jnp.einsum('qhgd,khd->hgqk', grouped, keys, precision=HIGH_PRECISION) * HEAD_WIDTH ** (-0.5)
    scores = lowered_backward(scores)
    row_index = jnp.arange(row_number, dtype=jnp.int32)
    allowed = (segment_labels[:, None] == segment_labels[None, :]) & (row_index[None, :] <= row_index[:, None])
    scores = jnp.where(allowed, scores, NEG)
    weights = low_precision(jax.nn.softmax(scores, axis=-1))
    mixed_heads = jnp.einsum('hgqk,khd->qhgd', weights, values, precision=HIGH_PRECISION)
    return mixed_heads.reshape(row_number, -1)

def layer_forward(block_tokens, attn_gain, wq, wk, wv, wo, mlp_gain, w_gate, w_up, w_down, segment_labels, cosine, sine_part):
    row_number = block_tokens.shape[0]
    head_groups = segment_labels.shape[0]
    normed_rows = low_precision(rms_norm(block_tokens, attn_gain))
    queries = lowered_backward(jnp.dot(normed_rows, wq, precision=HIGH_PRECISION)).reshape(row_number, QUERY_COUNT, HEAD_WIDTH)
    unrotated_keys = lowered_backward(jnp.dot(normed_rows, wk, precision=HIGH_PRECISION)).reshape(row_number, VALUE_HEADS, HEAD_WIDTH)
    lowered_values = low_precision(lowered_backward(jnp.dot(normed_rows, wv, precision=HIGH_PRECISION))).reshape(row_number, VALUE_HEADS, HEAD_WIDTH)
    rotated_queries = low_precision(rope_apply(queries, cosine, sine_part))
    rotated_keys = low_precision(rope_apply(unrotated_keys, cosine, sine_part))
    attended_rows = lax.map(jax.checkpoint(lambda split_pieces: grouped_attention(*split_pieces)), (rotated_queries.reshape(head_groups, -1, QUERY_COUNT, HEAD_WIDTH), rotated_keys.reshape(head_groups, -1, VALUE_HEADS, HEAD_WIDTH), lowered_values.reshape(head_groups, -1, VALUE_HEADS, HEAD_WIDTH), segment_labels))
    attended_rows = low_precision(lowered_backward(attended_rows.reshape(row_number, QUERY_COUNT * HEAD_WIDTH)))
    hidden = block_tokens + lowered_backward(jnp.dot(attended_rows, wo, precision=HIGH_PRECISION))
    normed_two = low_precision(rms_norm(hidden, mlp_gain))
    gate_proj = lowered_backward(jnp.dot(normed_two, w_gate, precision=HIGH_PRECISION))
    up_proj = lowered_backward(jnp.dot(normed_two, w_up, precision=HIGH_PRECISION))
    activation = low_precision(jax.nn.silu(gate_proj) * up_proj)
    return hidden + lowered_backward(jnp.dot(activation, w_down, precision=HIGH_PRECISION))

def reference(tokens, seq_lengths, attn_gain, wq, wk, wv, wo, mlp_gain, w_gate, w_up, w_down, cotangent):
    per_block = math.gcd(N_DP, 16)
    blocks = N_DP // per_block
    block_rows = per_block * GROUP_TOK
    weights = tuple((w.astype(jnp.float32) for w in (attn_gain, wq, wk, wv, wo, mlp_gain, w_gate, w_up, w_down)))
    all_tokens = tokens.astype(jnp.float32).reshape(blocks, block_rows, MODEL_WIDTH)
    all_grads = cotangent.astype(jnp.float32).reshape(blocks, block_rows, MODEL_WIDTH)
    all_lengths = seq_lengths.reshape(blocks, per_block, SEQS)

    def layout_of(lengths):
        return segment_layout(lengths, GROUP_TOK)

    def block_step(totals, block_item):
        block_tokens, block_grads, block_lengths = block_item
        segment_labels, positions = jax.vmap(layout_of)(block_lengths)
        cosine, sine_part = rotary_tables(positions.reshape(-1), HEAD_WIDTH)

        def forward_block(inputs, *params):
            return layer_forward(inputs, *params, segment_labels, cosine, sine_part)
        result, pullback = jax.vjp(forward_block, block_tokens, *weights)
        grads_here = pullback(block_grads)
        totals = tuple((prior + extra for prior, extra in zip(totals, grads_here[1:])))
        return (totals, (result, grads_here[0]))
    start_totals = tuple((jnp.zeros_like(w) for w in weights))
    totals, (results, input_grads) = lax.scan(block_step, start_totals, (all_tokens, all_grads, all_lengths))
    return (results.reshape(TOKENS, MODEL_WIDTH).astype(jnp.bfloat16), input_grads.reshape(TOKENS, MODEL_WIDTH).astype(jnp.bfloat16), totals[0], totals[1], totals[2], totals[3], totals[4], totals[5], totals[6], totals[7], totals[8])
```

```python
import functools
import math

import jax
import jax.numpy as jnp
from jax import lax
from jax.experimental import pallas as pl
from jax.experimental.pallas import tpu as pltpu
from jax.sharding import PartitionSpec as P

HEAD_WIDTH = 64
EPS = 1e-05
NEG = -1e30
PLANE = ("y", "x")
RING = 4
UP = [(i, (i + 1) % RING) for i in range(RING)]
DOWN = [(i, (i - 1) % RING) for i in range(RING)]
SWAP = [(0, 1), (1, 0)]
VMEM_LIMIT = 60 * 1024 * 1024


def rotary_tables(positions, head_size):
    freq_index = jnp.arange(head_size // 2, dtype=jnp.float32)
    inverse = 1.0 / 500000.0 ** (2.0 * freq_index / head_size)
    wavelen = 2.0 * math.pi / inverse
    smooth = (8192.0 / wavelen - 1.0) / 3.0
    blended = (1.0 - smooth) * inverse / 32.0 + smooth * inverse
    scaled = jnp.where(
        wavelen > 8192.0, inverse / 32.0, jnp.where(wavelen < 2048.0, inverse, blended)
    )
    angles = positions.astype(jnp.float32)[:, None] * scaled[None, :]
    return jnp.cos(angles), jnp.sin(angles)


def segment_starts(lengths, row_number):
    seq_ends = jnp.cumsum(lengths)
    row_index = jnp.arange(row_number, dtype=jnp.int32)
    passed = row_index[:, None] >= seq_ends[None, :]
    return jnp.max(jnp.where(passed, seq_ends[None, :], 0), axis=1)


def product(left_side, right_side):
    return jnp.dot(left_side, right_side, preferred_element_type=jnp.float32)


def contract_last(left_side, right_side):
    return lax.dot_general(
        left_side, right_side, (((1,), (1,)), ((), ())), preferred_element_type=jnp.float32
    )


def contract_first(left_side, right_side):
    return lax.dot_general(
        left_side, right_side, (((0,), (0,)), ((), ())), preferred_element_type=jnp.float32
    )


def rms_forward(row_values, gain_vector):
    scale_row = lax.rsqrt(jnp.mean(row_values * row_values, axis=-1, keepdims=True) + EPS)
    normal = row_values * scale_row
    return (normal, scale_row, (normal * gain_vector).astype(jnp.bfloat16))


def rms_backward(grad_out, normal, scale_row, gain_vector):
    grad_normal = grad_out * gain_vector
    inner_mean = jnp.mean(grad_normal * normal, axis=-1, keepdims=True)
    return scale_row * (grad_normal - normal * inner_mean)


def add_rows(left_side, right_side):
    return left_side.astype(jnp.float32) + right_side.astype(jnp.float32)


def after(value, *events):
    return lax.optimization_barrier((value, *events))[0]


def ring_scatter(pieces, axis, events=((), ()), marks=None):
    half = pieces[0].shape[0] // 2
    low, high = pieces[2] if isinstance(pieces[2], tuple) else jnp.split(pieces[2], 2, 0)
    from_low = after(lax.ppermute(low, axis, UP), *events[0])
    from_high = after(lax.ppermute(high, axis, DOWN), *events[0])
    first = jnp.concatenate(
        [add_rows(pieces[1][:half], from_low).astype(jnp.bfloat16), pieces[1][half:]], 0
    )
    third = jnp.concatenate(
        [pieces[3][:half], add_rows(pieces[3][half:], from_high).astype(jnp.bfloat16)], 0
    )
    if marks is not None:
        marks += [first, third]
    below = after(lax.ppermute(first, axis, UP), *events[1])
    above = after(lax.ppermute(third, axis, DOWN), *events[1])
    return add_rows(below, above) + pieces[0].astype(jnp.float32)


def ring_first(line, axis):
    return lax.ppermute(line, axis, UP), lax.ppermute(line, axis, DOWN)


def ring_rest(line, arrived, axis):
    half = line.shape[0] // 2
    below, above = arrived
    return [
        (0, 0, line),
        (1, 0, above),
        (3, 0, below),
        (2, 0, lax.ppermute(below[:half], axis, UP)),
        (2, half, lax.ppermute(above[half:], axis, DOWN)),
    ]


def ring_lines(line, arrived, axis):
    here = lax.axis_index(axis)
    whole = jnp.zeros((RING,) + line.shape, line.dtype)
    for r, start, part in ring_rest(line, arrived, axis):
        at = (lax.rem(here + r, RING), start) + (0,) * (line.ndim - 1)
        whole = lax.dynamic_update_slice(whole, part[None], at)
    return whole


def column_gather(block, arrived):
    own = ring_lines(block, arrived, ("zh", "zl")).reshape(RING * block.shape[0], -1)
    return own, lax.ppermute(own, "core", SWAP)


def pair_gather(block, *events):
    own = after(jnp.concatenate([block, lax.ppermute(block, "zl", SWAP)], 0), *events)
    return own, lax.ppermute(own, "core", SWAP)


def core_sum(own, other):
    return add_rows(own, lax.ppermute(other, "core", SWAP)).astype(jnp.bfloat16)


def column_pieces(summed):
    block = summed.shape[0] // RING
    here = lax.axis_index(("zh", "zl"))
    return [
        lax.dynamic_slice_in_dim(summed, lax.rem(here + r, RING) * block, block, 0)
        for r in range(RING)
    ]


def column_scatter(summed, events, marks):
    return ring_scatter(column_pieces(summed), ("zh", "zl"), events, marks)


def zl_halving(summed):
    rows = summed.reshape(2, 2, summed.shape[0] // 4, summed.shape[1])
    here = lax.axis_index("zl")
    mine = lax.dynamic_index_in_dim(rows, here, 1, keepdims=False)
    other = lax.dynamic_index_in_dim(rows, 1 - here, 1, keepdims=False)
    return mine, lax.ppermute(other, "zl", SWAP)


def zh_halving(rows, *events):
    here = lax.axis_index("zh")
    mine = lax.dynamic_index_in_dim(rows, here, 0, keepdims=False)
    other = lax.dynamic_index_in_dim(rows, 1 - here, 0, keepdims=False)
    return add_rows(mine, after(lax.ppermute(other, "zh", SWAP), *events))


def pair_scatter(summed):
    mine, partner = jnp.split(summed, 2, 0)
    return add_rows(mine, lax.ppermute(partner, "zl", SWAP))


def direct_scatter(pieces, axis, events=()):
    total = pieces[0].astype(jnp.float32)
    for r in range(1, RING):
        pairs = [(i, (i + r) % RING) for i in range(RING)]
        arrived = after(lax.ppermute(pieces[r], axis, pairs), *events)
        total = total + arrived.astype(jnp.float32)
    return total


def plane_scatter(pieces, y_first, events=((), (), ()), marks=None):
    first, second = ("y", "x") if y_first else ("x", "y")
    whole, low, high = pieces
    block = whole.shape[1] // RING
    pieces = [whole[0], whole[1], (low, high), whole[3]]
    mine = ring_scatter(pieces, first, events[:2], marks).astype(jnp.bfloat16)
    if marks is not None:
        marks.append(mine)
    parts = [
        lax.dynamic_slice_in_dim(mine, lax.rem(lax.axis_index(second) + r, RING) * block, block, 0)
        for r in range(RING)
    ]
    return direct_scatter(parts, second, events[2]).astype(jnp.bfloat16)


def quarter_turn(parts):
    core, high = lax.axis_index("core") == 1, lax.axis_index("zh") == 1
    parts = jnp.where(core, parts.reshape(2, 2, *parts.shape[1:])[:, ::-1].reshape(parts.shape), parts)
    return jnp.where(high, jnp.concatenate([parts[2:], parts[:2]], 0), parts)


def quarter_exchange(parts):
    near = quarter_turn(parts)
    return quarter_arrived([near[mask : mask + 1] for mask in range(4)])


def quarter_arrived(near):
    arrived = [near[0]]
    for mask in range(1, 4):
        pairs = [(i, i ^ mask) for i in range(4)]
        arrived.append(lax.ppermute(near[mask], ("zh", "core"), pairs))
    return quarter_turn(jnp.concatenate(arrived, 0))


def quarter_scatter(rows):
    count = rows.shape[0] // 4
    here = lax.axis_index(("zh", "core"))
    arrived = []
    for mask in range(4):
        place = jnp.bitwise_xor(here, mask) * count
        part = lax.dynamic_slice_in_dim(rows, place, count, 0)
        if mask:
            part = lax.ppermute(part, ("zh", "core"), [(i, i ^ mask) for i in range(4)])
        arrived.append(part)
    return arrived


def quarters(*shards):
    split = [w.reshape(w.shape[0], 4, -1) for w in shards]
    return jnp.swapaxes(jnp.concatenate(split, 2), 0, 1)


def half_turn(values):
    width = values.shape[1]
    quarter = HEAD_WIDTH // 2
    lane = lax.broadcasted_iota(jnp.int32, values.shape, 1)
    ahead = pltpu.roll(values, width - quarter, 1)
    behind = pltpu.roll(values, quarter, 1)
    return jnp.where(lane % HEAD_WIDTH < quarter, ahead, behind)


def wide_tables(cos_ref, sin_ref, width):
    copies = -(-width // cos_ref.shape[2])
    cosine = jnp.concatenate([cos_ref[0]] * copies, 1)[:, :width]
    sine_part = jnp.concatenate([sin_ref[0]] * copies, 1)[:, :width]
    turns = lax.broadcasted_iota(jnp.int32, cosine.shape, 1) < width - HEAD_WIDTH
    return jnp.where(turns, cosine, 1.0), jnp.where(turns, sine_part, 0.0)


def head_of(values, head):
    return values[:, head * HEAD_WIDTH : (head + 1) * HEAD_WIDTH]


def head_probs(queries, keys, allowed):
    scores = contract_last(queries, keys) * HEAD_WIDTH ** (-0.5)
    scores = jnp.where(allowed, scores, NEG)
    exp_scores = jnp.exp(scores - jnp.max(scores, axis=-1, keepdims=True))
    return exp_scores / jnp.sum(exp_scores, axis=-1, keepdims=True)


def allowed_of(starts):
    rows = starts.shape[0]
    row = lax.broadcasted_iota(jnp.int32, (rows, rows), 0)
    column = lax.broadcasted_iota(jnp.int32, (rows, rows), 1)
    return (column <= row) & (column >= starts)


def pair_rows(zl_ref, first_ref, second_ref, part):
    block = first_ref.shape[0]
    place = (1 - 2 * part) * zl_ref[0] + part
    return pl.ds(pl.multiple_of(place * block, block), block)


def accumulate(total_ref, part):
    @pl.when(pl.program_id(0) == 0)
    def _():
        total_ref[...] = part

    @pl.when(pl.program_id(0) > 0)
    def _():
        total_ref[...] += part


def attend_kernel(
    heads, zl_ref, first_ref, second_ref, weights_ref, cos_ref, sin_ref, start_ref,
    qkv_ref, probs_ref, mixed_ref, out_ref, total_ref,
):
    block = first_ref.shape[0]
    qkv_width = qkv_ref.shape[2]
    rows = jnp.concatenate([first_ref[...], second_ref[...]], 0)
    raw = product(rows, weights_ref[:, :qkv_width])
    cosine, sine_part = wide_tables(cos_ref, sin_ref, qkv_width)
    turned = (raw * cosine + half_turn(raw) * sine_part).astype(jnp.bfloat16)
    qkv_ref[0] = turned
    keys, values = head_of(turned, heads), head_of(turned, heads + 1)
    allowed = allowed_of(start_ref[0])
    mixed = []
    for head in range(heads):
        probs = head_probs(head_of(turned, head), keys, allowed).astype(jnp.bfloat16)
        probs_ref[0, head] = probs
        mixed.append(product(probs, values).astype(jnp.bfloat16))
    mixed = jnp.concatenate(mixed, 1)
    accumulate(total_ref, contract_last(mixed, weights_ref[:, qkv_width:]))
    for part in range(2):
        place = pair_rows(zl_ref, first_ref, second_ref, part)
        rows_here = slice(part * block, (part + 1) * block)
        mixed_ref[place, :] = mixed[rows_here]

        @pl.when(pl.program_id(0) == pl.num_programs(0) - 1)
        def _():
            out_ref[place, :] = total_ref[rows_here, :].astype(jnp.bfloat16)


def group_back(heads, rows, weights_ref, cos_ref, sin_ref, qkv_ref, probs_ref):
    qkv_width = qkv_ref.shape[2]
    grad_mixed = product(rows, weights_ref[:, qkv_width:]).astype(jnp.bfloat16)
    turned = qkv_ref[0]
    keys, values = head_of(turned, heads), head_of(turned, heads + 1)
    scale = HEAD_WIDTH ** (-0.5)
    parts, grad_keys, grad_values = [], 0.0, 0.0
    for head in range(heads):
        queries, grad_head = head_of(turned, head), head_of(grad_mixed, head)
        probs = probs_ref[0, head]
        grad_probs = contract_last(grad_head, values)
        wide = probs.astype(jnp.float32)
        inner = jnp.sum(wide * grad_probs, axis=-1, keepdims=True)
        grad_scores = (wide * (grad_probs - inner)).astype(jnp.bfloat16)
        parts.append(product(grad_scores, keys) * scale)
        grad_keys = grad_keys + contract_first(grad_scores, queries)
        grad_values = grad_values + contract_first(probs, grad_head)
    parts = jnp.concatenate([*parts, grad_keys * scale, grad_values], 1)
    cosine, sine_part = wide_tables(cos_ref, sin_ref, qkv_width)
    grad_qkv = (parts * cosine + half_turn(parts * sine_part)).astype(jnp.bfloat16)
    return grad_qkv, contract_last(grad_qkv, weights_ref[:, :qkv_width])


def attend_back_kernel(heads, zl_ref, weights_ref, *refs):
    groups = (refs[:6], refs[6:12])
    outputs, totals = (refs[12:14], refs[14:16]), refs[16:]
    found = []
    for first_ref, second_ref, *rest in groups:
        rows = jnp.concatenate([first_ref[...], second_ref[...]], 0)
        found.append(group_back(heads, rows, weights_ref, *rest))
    for group, (grad_qkv, part) in enumerate(found):
        first_ref, second_ref = groups[group][:2]
        block = first_ref.shape[0]
        grad_qkv_ref, out_ref = outputs[group]
        total_ref = totals[group]
        accumulate(total_ref, part)
        for half in range(2):
            place = pair_rows(zl_ref, first_ref, second_ref, half)
            rows_here = slice(half * block, (half + 1) * block)
            grad_qkv_ref[place, :] = grad_qkv[rows_here]

            @pl.when(pl.program_id(0) == pl.num_programs(0) - 1)
            def _():
                out_ref[place, :] = total_ref[rows_here, :].astype(jnp.bfloat16)


def cost(micros):
    return pl.CostEstimate(
        flops=int(micros * 1.15e9), bytes_accessed=int(micros * 3e6), transcendentals=0
    )


def attention_specs(rows, tables, qkv_width, heads):
    count, width = rows.shape
    block = count // 2
    halves = [
        pl.BlockSpec((block, width), lambda c, zl: (zl[0], 0)),
        pl.BlockSpec((block, width), lambda c, zl: (1 - zl[0], 0)),
    ]
    tables = [pl.BlockSpec((1,) + t.shape[1:], lambda c, zl: (0, 0, 0)) for t in tables]
    by_head = pl.BlockSpec((1, count, qkv_width), lambda c, zl: (c, 0, 0))
    by_probs = pl.BlockSpec((1, heads, count, count), lambda c, zl: (c, 0, 0, 0))
    return halves, tables, [by_head, by_probs]


def attend(zl, rows, weights, tables, heads):
    count, width = rows.shape
    qkv_width, mixed_width = (heads + 2) * HEAD_WIDTH, heads * HEAD_WIDTH
    columns = qkv_width + mixed_width
    key_heads = weights.shape[1] // columns
    halves, table_specs, saved = attention_specs(rows, tables, qkv_width, heads)
    return pl.pallas_call(
        functools.partial(attend_kernel, heads),
        grid_spec=pltpu.PrefetchScalarGridSpec(
            num_scalar_prefetch=1,
            grid=(key_heads,),
            in_specs=[*halves, pl.BlockSpec((width, columns), lambda c, zl: (0, c)), *table_specs],
            out_specs=[
                *saved,
                pl.BlockSpec((count, mixed_width), lambda c, zl: (0, c)),
                pl.BlockSpec((count, width), lambda c, zl: (0, 0)),
            ],
            scratch_shapes=[pltpu.VMEM((count, width), jnp.float32)],
        ),
        out_shape=[
            jax.ShapeDtypeStruct((key_heads, count, qkv_width), jnp.bfloat16),
            jax.ShapeDtypeStruct((key_heads, heads, count, count), jnp.bfloat16),
            jax.ShapeDtypeStruct((count, key_heads * mixed_width), jnp.bfloat16),
            jax.ShapeDtypeStruct((count, width), jnp.bfloat16),
        ],
        compiler_params=pltpu.CompilerParams(vmem_limit_bytes=VMEM_LIMIT),
        cost_estimate=cost(8),
        name="attend",
    )(zl, rows, rows, weights, *tables)


def attend_back(zl, weights, groups, heads):
    qkv_width = (heads + 2) * HEAD_WIDTH
    columns = qkv_width + heads * HEAD_WIDTH
    key_heads = weights.shape[1] // columns
    in_specs, out_specs, out_shape, scratch, operands = [], [], [], [], []
    for rows, tables, saved in groups:
        count, width = rows.shape
        in_specs += sum(attention_specs(rows, tables, qkv_width, heads), [])
        operands += [rows, rows, *tables, *saved]
        out_specs += [
            pl.BlockSpec((count, qkv_width), lambda c, zl: (0, c)),
            pl.BlockSpec((count, width), lambda c, zl: (0, 0)),
        ]
        out_shape += [
            jax.ShapeDtypeStruct((count, key_heads * qkv_width), jnp.bfloat16),
            jax.ShapeDtypeStruct((count, width), jnp.bfloat16),
        ]
        scratch.append(pltpu.VMEM((count, width), jnp.float32))
    return pl.pallas_call(
        functools.partial(attend_back_kernel, heads),
        grid_spec=pltpu.PrefetchScalarGridSpec(
            num_scalar_prefetch=1,
            grid=(key_heads,),
            in_specs=[pl.BlockSpec((width, columns), lambda c, zl: (0, c)), *in_specs],
            out_specs=out_specs,
            scratch_shapes=scratch,
        ),
        out_shape=out_shape,
        compiler_params=pltpu.CompilerParams(vmem_limit_bytes=VMEM_LIMIT),
        cost_estimate=cost(20),
        name="attend_back",
    )(zl, weights, *operands)


def feed_kernel(
    rows_hbm, cot_hbm, weights_hbm, act_hbm, grads_hbm, out_hbm,
    rows, cot, weights, act, grads, out, arrived, left,
):
    hidden = act.shape[1]

    def columns(part):
        at = pl.ds(part * hidden, hidden)
        return pltpu.make_async_copy(
            weights_hbm.at[:, at], weights.at[:, at], arrived.at[part]
        )

    gate_copy, up_copy, down_copy = [columns(part) for part in range(3)]
    rows_copy = pltpu.make_async_copy(rows_hbm, rows, arrived.at[3])
    cot_copy = pltpu.make_async_copy(cot_hbm, cot, arrived.at[4])
    rows_copy.start()
    gate_copy.start()
    rows_copy.wait()
    gate_copy.wait()
    up_copy.start()
    cot_copy.start()
    down_copy.start()
    gate_proj = product(rows[...], weights[:, :hidden])
    sigmoid = 1.0 / (1.0 + jnp.exp(-gate_proj))
    up_copy.wait()
    up_proj = product(rows[...], weights[:, hidden : 2 * hidden])
    silu = gate_proj * sigmoid
    act[...] = (silu * up_proj).astype(jnp.bfloat16)
    cot_copy.wait()
    down_copy.wait()
    grad_act = product(cot[...], weights[:, 2 * hidden :])
    grads[:, :hidden] = (
        grad_act * up_proj * sigmoid * (1.0 + gate_proj * (1.0 - sigmoid))
    ).astype(jnp.bfloat16)
    grads[:, hidden:] = (grad_act * silu).astype(jnp.bfloat16)
    leaving = [
        pltpu.make_async_copy(act, act_hbm, left.at[0]),
        pltpu.make_async_copy(grads, grads_hbm, left.at[1]),
        pltpu.make_async_copy(out, out_hbm, left.at[2]),
    ]
    leaving[0].start()
    leaving[1].start()
    out[...] = contract_last(grads[...], weights[:, : 2 * hidden]).astype(jnp.bfloat16)
    leaving[2].start()
    for copy in leaving:
        copy.wait()


def feed(rows, cot_rows, weights):
    count, width = rows.shape
    hidden = weights.shape[1] // 3
    shapes = [(count, hidden), (count, 2 * hidden), (count, width)]
    shapes_in = [(count, width), (count, width), weights.shape]
    anywhere = pl.BlockSpec(memory_space=pl.ANY)
    return pl.pallas_call(
        feed_kernel,
        in_specs=[anywhere] * 3,
        out_specs=[anywhere] * 3,
        out_shape=[jax.ShapeDtypeStruct(shape, jnp.bfloat16) for shape in shapes],
        scratch_shapes=[
            *[pltpu.VMEM(shape, jnp.bfloat16) for shape in shapes_in + shapes],
            pltpu.SemaphoreType.DMA((5,)),
            pltpu.SemaphoreType.DMA((3,)),
        ],
        compiler_params=pltpu.CompilerParams(vmem_limit_bytes=VMEM_LIMIT),
        cost_estimate=cost(15),
        name="feed",
    )(rows, cot_rows, weights)


def down_kernel(act_ref, down_ref, out_ref):
    out_ref[...] = contract_last(act_ref[...], down_ref[...]).astype(jnp.bfloat16)


def down_product(act, weights):
    count, hidden = act.shape
    model = weights.shape[0]
    tile = model // RING
    return pl.pallas_call(
        down_kernel,
        grid=(RING,),
        in_specs=[
            pl.BlockSpec((count, hidden), lambda t: (0, 0)),
            pl.BlockSpec((tile, hidden), lambda t: (t, 2)),
        ],
        out_specs=pl.BlockSpec((count, tile), lambda t: (0, t)),
        out_shape=jax.ShapeDtypeStruct((count, model), jnp.bfloat16),
        compiler_params=pltpu.CompilerParams(vmem_limit_bytes=VMEM_LIMIT),
        cost_estimate=cost(6),
        name="down_product",
    )(act, weights)


def swapped(condition, first, second):
    return jnp.where(condition, second, first), jnp.where(condition, first, second)


def row_sums(ref, grads):
    return jnp.sum(ref[...].astype(jnp.float32) * grads, axis=1, keepdims=True)


def feed_end_kernel(place_ref, *refs):
    arrived, (gate_w_ref, up_w_ref, gate_ref, up_ref, down_ref, gain_ref) = refs[:4], refs[4:]
    parts = [ref[...].astype(jnp.float32) for ref in arrived]
    core, high = place_ref[1] == 1, place_ref[0] == 1
    parts[0], parts[1] = swapped(core, parts[0], parts[1])
    parts[2], parts[3] = swapped(core, parts[2], parts[3])
    parts[0], parts[2] = swapped(high, parts[0], parts[2])
    parts[1], parts[3] = swapped(high, parts[1], parts[3])
    width = gate_ref.shape[1] // 4
    for place, out_ref in enumerate((down_ref, gate_ref, up_ref)):
        for quarter in range(4):
            at = quarter * width
            out_ref[:, at : at + width] = parts[quarter][:, place * width : (place + 1) * width]
    gain = row_sums(gate_w_ref, gate_ref[...]) + row_sums(up_w_ref, up_ref[...])
    gain_ref[...] = jnp.broadcast_to(gain, gain_ref.shape)


def attn_end_kernel(
    place_ref, near, core_near, high_near, far,
    query_w_ref, key_w_ref, value_w_ref,
    query_ref, key_ref, value_ref, output_ref, gain_ref,
):
    mine = near[...].astype(jnp.float32) + high_near[...].astype(jnp.float32)
    other = core_near[...].astype(jnp.float32) + far[...].astype(jnp.float32)
    parts = swapped(place_ref[1] == 1, mine, other)
    wide, narrow = query_ref.shape[1] // 4, key_ref.shape[1] // 4
    head = 2 * (wide + narrow)
    edges = (0, wide, wide + narrow, wide + 2 * narrow, head)
    outs = (query_ref, key_ref, value_ref, output_ref)
    for out_ref, low, high in zip(outs, edges[:-1], edges[1:]):
        pieces = [part[:, c * head + low : c * head + high] for part in parts for c in range(2)]
        out_ref[...] = jnp.concatenate(pieces, 1)
    gain = row_sums(query_w_ref, query_ref[...]) + row_sums(key_w_ref, key_ref[...])
    gain = gain + row_sums(value_w_ref, value_ref[...])
    gain_ref[...] = jnp.broadcast_to(gain, gain_ref.shape)


def end_call(kernel, name, place, arrived, weights, widths):
    rows = arrived[0].shape[0]
    out_shape = [jax.ShapeDtypeStruct((rows, width), jnp.float32) for width in (*widths, 128)]
    smem = pl.BlockSpec(memory_space=pltpu.SMEM)
    vmem = pl.BlockSpec(memory_space=pltpu.VMEM)
    return pl.pallas_call(
        kernel,
        in_specs=[smem] + [vmem] * (len(arrived) + len(weights)),
        out_specs=[vmem] * len(out_shape),
        out_shape=out_shape,
        compiler_params=pltpu.CompilerParams(vmem_limit_bytes=VMEM_LIMIT),
        cost_estimate=cost(3),
        name=name,
    )(place, *arrived, *weights)


def plane_kernel(parts, blocks, place_ref, *refs):
    out_ref, low_ref, high_ref = refs[-3:]
    half = low_ref.shape[0]
    edge = 0
    for part in range(parts):
        sources = refs[part * 2 * (blocks + 1) : (part + 1) * 2 * (blocks + 1)]
        total = 0.0
        for side in range(2):
            left = [ref[...] for ref in sources[side * blocks : (side + 1) * blocks]]
            right = sources[2 * blocks + side][...]
            total = total + contract_first(jnp.concatenate(left, 1), right)
        total = total.astype(jnp.bfloat16)
        columns = slice(edge, edge + total.shape[1])
        out_ref[0, :, columns] = total

        @pl.when(pl.program_id(0) == RING // 2)
        def _(total=total, columns=columns):
            low_ref[:, columns] = total[:half]
            high_ref[:, columns] = total[half:]

        edge += total.shape[1]


def plane_products(place, y_first, parts):
    operands, specs, total = [], [], 0
    blocks = 1 if y_first else RING
    for lefts, rights, split, index in parts:
        for left in lefts:
            width = left.shape[1] // (RING * RING)
            for other in range(blocks):
                operands.append(left)

                def columns(s, place, other=other):
                    if y_first:
                        return (0, (place[0] + s) % RING)
                    return (0, other * RING + (place[1] + s) % RING)

                specs.append(pl.BlockSpec((left.shape[0], RING // blocks * width), columns))
        for right in rights:
            operands.append(right)
            columns = right.shape[1] // split
            specs.append(
                pl.BlockSpec((right.shape[0], columns), lambda s, place, index=index: (0, index))
            )
        total += columns
    out = jax.ShapeDtypeStruct((RING, RING * width, total), jnp.bfloat16)
    far = jax.ShapeDtypeStruct((RING * width // 2, total), jnp.bfloat16)
    far_spec = pl.BlockSpec(far.shape, lambda s, place: (0, 0))
    return pl.pallas_call(
        functools.partial(plane_kernel, len(parts), blocks),
        grid_spec=pltpu.PrefetchScalarGridSpec(
            num_scalar_prefetch=1,
            grid=(RING,),
            in_specs=specs,
            out_specs=[
                pl.BlockSpec((1, RING * width, total), lambda s, place: (s, 0, 0)),
                far_spec,
                far_spec,
            ],
        ),
        out_shape=[out, far, far],
        compiler_params=pltpu.CompilerParams(vmem_limit_bytes=VMEM_LIMIT),
        cost_estimate=cost(6),
        name="plane_products",
    )(place, *operands)


def model_kernel(left_own, left_other, right_own, right_other, *refs):
    total = contract_first(left_own[...], right_own[...])
    refs[-1][...] = (total + contract_first(left_other[...], right_other[...])).astype(jnp.bfloat16)


def model_products(lefts, rights, width, first, total=None):
    count, model = lefts[0].shape
    slab = model // RING
    columns = rights[0].shape[1] // width
    left = pl.BlockSpec((count, slab), lambda s, j: (0, s))
    right = pl.BlockSpec((count, width), lambda s, j: (0, j))
    out = jax.ShapeDtypeStruct((model, 3 * width), jnp.bfloat16)
    held = () if total is None else (total,)
    return pl.pallas_call(
        model_kernel,
        grid=(RING, columns),
        in_specs=[left, left, right, right] + [pl.BlockSpec(memory_space=pl.ANY) for _ in held],
        out_specs=pl.BlockSpec((slab, width), lambda s, j: (s, first + j)),
        out_shape=out,
        input_output_aliases={4: 0} if held else {},
        compiler_params=pltpu.CompilerParams(vmem_limit_bytes=VMEM_LIMIT),
        cost_estimate=cost(8 * columns),
        name="model_products",
    )(*lefts, *rights, *held)


def on_device(
    tokens, seq_lengths, attn_gain, wq, wk, wv, wo, mlp_gain, w_gate, w_up, w_down, cotangent
):
    wo_rows, down_rows = wo.T, w_down.T
    rows = wq.shape[0]
    key_width = wk.shape[1] // 4
    query_width = wq.shape[1] // 4
    attn_width = 2 * query_width + 2 * key_width
    hidden_width = w_gate.shape[1] // 4
    heads = query_width // HEAD_WIDTH
    core = lax.axis_index("core")

    def core_columns(which):
        pieces = []
        for c in range(2):
            for w in (wq, wk, wv, wo_rows):
                width = w.shape[1] // 4
                pieces.append(lax.dynamic_slice_in_dim(w, (2 * which + c) * width, width, 1))
        return jnp.concatenate(pieces, 1)[None]

    mine, other = core_columns(core), core_columns(1 - core)
    attn_block = quarter_arrived([mine, other, mine, other]).reshape(4 * rows, -1)
    full_attn = lax.all_gather(attn_block, PLANE, axis=0, tiled=True)

    residual = tokens.astype(jnp.float32)
    normal_one, scale_one, low_one = rms_forward(residual, attn_gain)
    one_own, one_other = pair_gather(low_one)
    feed_block = quarter_exchange(after(quarters(w_gate, w_up, down_rows), one_own))
    feed_block = feed_block.reshape(4 * rows, -1)
    full_feed = lax.all_gather(feed_block, PLANE, axis=0, tiled=True)
    cot_block = after(cotangent, one_own)
    cot_own, cot_other = column_gather(cot_block, ring_first(cot_block, ("zh", "zl")))

    lengths = after(seq_lengths, attn_block)
    lengths = jnp.concatenate([lengths, lax.ppermute(lengths, "core", SWAP)], 0)
    group_rows = one_own.shape[0]
    starts = jax.vmap(lambda one: segment_starts(one, group_rows))(lengths)
    positions = jnp.arange(group_rows, dtype=jnp.int32)[None] - starts
    cosine, sine_part = jax.vmap(lambda one: rotary_tables(one, HEAD_WIDTH))(positions)
    cosine = jnp.concatenate([cosine] * 4, 2)
    sine_part = jnp.concatenate([-sine_part, sine_part] * 2, 2)
    tables = (cosine, sine_part, starts[:, :, None])
    own_tables, other_tables = [tuple(t[i : i + 1] for t in tables) for i in (0, 1)]
    zl = lax.axis_index("zl").astype(jnp.int32).reshape(1)
    place = jnp.stack([lax.axis_index("y"), lax.axis_index("x")]).astype(jnp.int32)

    *saved_other, mixed_other, out_other = attend(zl, one_other, full_attn, other_tables, heads)
    own_rows = after(one_own, out_other)
    *saved_own, mixed_own, out_own = attend(zl, own_rows, full_attn, own_tables, heads)
    pair_sum = after(core_sum(out_own, out_other), cot_own)
    hidden = residual + pair_scatter(pair_sum)
    normal_two, scale_two, low_two = rms_forward(hidden, mlp_gain)
    two_own, two_other = column_gather(low_two, ring_first(low_two, ("zh", "zl")))

    act_other, grads_other, out_other = feed(two_other, cot_other, full_feed)
    act_own, grads_own, out_own = feed(after(two_own, out_other), cot_own, full_feed)
    feed_sum = core_sum(out_own, out_other)
    marks = []
    feed_total = model_products(
        (cot_own, cot_other), (after(act_own, feed_sum), act_other), hidden_width, 0
    )
    grad_normal_two = column_scatter(feed_sum, ((feed_total,), ()), marks)
    feed_total = model_products(
        (two_own, two_other), (after(grads_own, *marks), grads_other), hidden_width, 1, feed_total
    )

    grad_mid = rms_backward(grad_normal_two, normal_two, scale_two, mlp_gain)
    grad_hidden = cotangent.astype(jnp.float32) + grad_mid
    low_mid = after(grad_hidden.astype(jnp.bfloat16), feed_total)
    mlp_other = down_product(after(act_other, low_mid), full_feed)
    mlp_own = down_product(after(act_own, low_mid), full_feed)
    mid_own, mid_other = pair_gather(low_mid, mlp_own, mlp_other)
    groups = ((mid_own, own_tables[:2], saved_own), (mid_other, other_tables[:2], saved_other))
    grad_own, out_own, grad_other, out_other = attend_back(zl, full_attn, groups, heads)
    pair_sum = core_sum(out_own, out_other)

    attn_pieces, event = [], out_own
    for index, y_first in ((0, True), (1, False)):
        parts = (
            ((one_own, one_other), (after(grad_own, event), grad_other), 2, index),
            ((mid_own, mid_other), (mixed_own, mixed_other), 2, index),
        )
        attn_pieces.append(plane_products(place, y_first, parts))
        event = attn_pieces[0][0]
    feed_total = after(feed_total, grad_normal_two)
    feed_sum = lax.psum_scatter(feed_total, PLANE, scatter_dimension=0, tiled=True)
    grad_normal_one = pair_scatter(pair_sum)
    feed_parts = quarter_scatter(feed_sum)

    marks, second_marks = [], []
    events = ((grad_normal_one,), (), (feed_sum,))
    first_sum = plane_scatter(attn_pieces[0], True, events, marks)
    second_pieces = [after(piece, *marks[:2]) for piece in attn_pieces[1]]
    mlp_sum = core_sum(after(mlp_own, *marks[:2]), mlp_other)
    mlp_half, arrived = zl_halving(mlp_sum)
    mlp_half = add_rows(mlp_half, arrived).astype(jnp.bfloat16)
    events = ((), (marks[2], mlp_half), tuple(feed_parts))
    second_sum = plane_scatter(second_pieces, False, events, second_marks)
    mlp_out = zh_halving(mlp_half)
    layer_out = (hidden + mlp_out).astype(jnp.bfloat16)
    grad_first = rms_backward(grad_normal_one, normal_one, scale_one, attn_gain)
    tokens_grad = (grad_hidden + grad_first).astype(jnp.bfloat16)

    attn_sum = after(jnp.concatenate([first_sum, second_sum], 1), layer_out)
    attn_parts = quarter_scatter(attn_sum)
    quarter = jnp.stack([lax.axis_index("zh"), lax.axis_index("core")]).astype(jnp.int32)
    gate_shard, up_shard, down_shard, feed_gain = end_call(
        feed_end_kernel, "feed_end", quarter, feed_parts, (w_gate, w_up), 3 * (w_gate.shape[1],)
    )
    query_shard, key_shard, value_shard, output_shard, attn_gain_sum = end_call(
        attn_end_kernel,
        "attn_end",
        quarter,
        attn_parts,
        (wq, wk, wv),
        (wq.shape[1], wk.shape[1], wv.shape[1], wo.shape[0]),
    )
    gains = jnp.stack([attn_gain_sum[:, 0], feed_gain[:, 0]])
    gains = gains + lax.ppermute(gains, "zl", SWAP)
    start = lax.axis_index(("y", "x", "zh", "core")) * rows
    own_gains = lax.dynamic_slice_in_dim(jnp.stack([attn_gain, mlp_gain]), start, rows, 1)
    gains = gains / own_gains
    return (
        layer_out,
        tokens_grad,
        gains[0],
        query_shard,
        key_shard,
        value_shard,
        output_shard.T,
        gains[1],
        gate_shard,
        up_shard,
        down_shard.T,
    )


def solution(mesh):
    fine = jax.sharding.Mesh(
        mesh.devices.reshape(RING, RING, 2, 2, 2), ("y", "x", "zh", "core", "zl")
    )
    dp, tensor = ("y", "x", "zh", "core"), "zl"
    rows, split, joint = P(dp + (tensor,), None), P(dp, tensor), P(tensor, dp)
    in_specs = (
        rows, P(dp, None), P(), split, split, split, joint, P(), split, split, joint, rows,
    )
    out_specs = (
        rows, rows, P(dp), split, split, split, joint, P(dp), split, split, joint,
    )
    return jax.shard_map(
        on_device, mesh=fine, in_specs=in_specs, out_specs=out_specs, check_vma=False
    )
```
